128 devices in a mesh: pre: 32 (over y, x, core), suf: 4 (over z).
Axes of the slice: x: 4, y: 4, z: 4, core: 2. Of those that a mesh axis runs over, the one named last changes fastest.
Arguments:
- values: bfloat16 [128, 192, 128, 128], P(('pre', 'suf'))
- block_rows: int32 [128, 192], P(('pre', 'suf')), may hold values from 0 to 15, as said below
- block_cols: int32 [128, 192], P(('pre', 'suf')), may hold values from 0 to 15
- block_count: int32 [128], P(('pre', 'suf')), may hold values from 1 to 192, as said below
- test_matrix: bfloat16 [8192, 512], P(('suf', 'pre')), may hold values from -6 to 6
Outputs:
- prefix_basis: float32 [65536, 512], P(('pre', 'suf'))
- suffix_basis: float32 [8192, 512], P(('suf', 'pre'))
The draws below stay inside these ranges and needn't reach their ends.
Inputs may be any that keep to these rules, and one draw needn't show every extreme that they name: The live (block_rows, block_cols) pairs of one list are distinct. `block_count`: the live slots of a list are its first ones; some list has all 192 slots live.
All inputs are finite; a program needn't handle non-finite values.
Results may differ from the reference program's by a relative error of at most 0.003.
Values may be sent and summed in bfloat16 or wider, within the bound.
No kernel may reach another device: no remote copies, remote signals or barrier semaphores. Data moves between devices by JAX's collectives and lax.ppermute only.
A program may use at most 128 MiB of HBM per device.

```python
import math
import jax
import jax.numpy as jnp
from jax import lax

BLK = 128
RANK = 512
PB = 16
SB = 16
CAP = 192
SUF_PARTS = 4
LISTS = 128
PRE_BLOCKS = 512
SUF_BLOCKS = 64
PREFIXES = 65536
SUFFIXES = 8192


def pair_positions(key):
    keys = jax.random.split(key, LISTS)

    def one_list(single):
        return jax.random.permutation(single, PB * SB)[:CAP]
    return jax.vmap(one_list)(keys).astype(jnp.int32)


def draw_block_rows(key, part):
    positions = pair_positions(key)
    return (positions // SB).astype(jnp.int32)


def draw_block_cols(key, part):
    positions = pair_positions(key)
    return (positions % SB).astype(jnp.int32)


def draw_block_count(key, part):
    key = jax.random.fold_in(key, 3)
    first_key, second_key = jax.random.split(key)
    lowest = max(CAP // 4, 1)
    counts = jax.random.randint(first_key, (LISTS,), lowest, CAP + 1)
    fullest = jax.random.randint(second_key, (), 0, LISTS)
    counts = jnp.where(jnp.arange(LISTS) == fullest, CAP, counts)
    return counts.astype(jnp.int32)


def draw_values(key, part):
    positions = pair_positions(key)
    key = jax.random.fold_in(key, 5)
    entry_key = jax.random.fold_in(key, 0)
    scale_key = jax.random.fold_in(key, 1)
    core_key = jax.random.fold_in(key, 3)
    left_key = jax.random.fold_in(key, 4)
    right_key = jax.random.fold_in(key, 5)
    states = max(1, min(BLK, 7 * RANK // (8 * SUF_BLOCKS)))
    lists = jnp.arange(LISTS, dtype=jnp.int32)[:, None]
    prefix_ids = (lists // SUF_PARTS * PB + positions // SB).astype(jnp.int32)
    suffix_ids = (lists % SUF_PARTS * SB + positions % SB).astype(jnp.int32)
    left_table = jax.random.normal(left_key, (PRE_BLOCKS, BLK, states), jnp.float32)
    right_table = jax.random.normal(right_key, (SUF_BLOCKS, BLK, states), jnp.float32)
    left = left_table[prefix_ids]
    right = right_table[suffix_ids]
    shape = (LISTS, CAP, BLK, BLK)
    cores = jnp.clip(jax.random.normal(core_key, (LISTS, CAP, states), jnp.float32), -6.0, 6.0)
    entries = jnp.clip(jax.random.normal(entry_key, shape, jnp.float32), -6.0, 6.0)
    spread = jax.random.uniform(scale_key, (LISTS, CAP, 1, 1), jnp.float32, 0.0, math.log(10.0))
    noise_level = 0.009
    structured = jnp.zeros(shape, jnp.float32)
    for state in range(states):
        outer = left[:, :, :, state, None] * right[:, :, None, :, state]
        structured = structured + cores[:, :, state, None, None] * outer
    structured = structured * (1.0 / math.sqrt(states))
    noise = noise_level * entries * jnp.exp(spread)
    trend = math.log(3.0) * jnp.arange(LISTS, dtype=jnp.float32) / (LISTS - 1)
    scaled = (structured + noise) * jnp.exp(-trend[:, None, None, None])
    return scaled.astype(jnp.bfloat16)


def levels(stream_key, extent, cuts, smallest, high):
    gain, own = 1.0, jax.random.fold_in(stream_key, 6)
    for position, blocks in cuts:
        heights = jnp.exp(jax.random.uniform(jax.random.fold_in(own, position), (blocks,), jnp.float32, smallest / len(cuts), high / len(cuts)))
        gain = gain * jnp.repeat(heights, extent[position] // blocks).reshape([-1 if axis == position else 1 for axis in range(len(extent))])
    return gain


def scatter_about(rng, dims, width, reach, shards=(), kind=jnp.bfloat16):
    level = levels(rng, dims, shards, -0.22, 0.18) if shards else 1.0
    values = jax.random.normal(rng, dims, jnp.float32) * width * level
    return jnp.minimum(jnp.maximum(values, -reach), reach).astype(kind)


def setup_inputs(seed: int = 0) -> dict:
    key_of = jax.random.split(jax.random.key(seed), 6)
    return {
        "values": draw_values(jax.random.fold_in(key_of[5], 71), 0),
        "block_rows": draw_block_rows(jax.random.fold_in(key_of[5], 71), 0),
        "block_cols": draw_block_cols(jax.random.fold_in(key_of[5], 71), 0),
        "block_count": draw_block_count(jax.random.fold_in(key_of[5], 71), 0),
        "test_matrix": scatter_about(key_of[4], (SUFFIXES, RANK), 1.0, 6.0, ((0, 128),)),
    }


highest = lax.Precision.HIGHEST

def block_places(block_rows, block_cols):
    lists = jnp.arange(LISTS, dtype=jnp.int32)
    prefix_ids = (lists // SUF_PARTS)[:, None] * PB + block_rows
    suffix_ids = (lists % SUF_PARTS)[:, None] * SB + block_cols
    return (prefix_ids.astype(jnp.int32), suffix_ids.astype(jnp.int32))

def block_product(values, take_ids, place_ids, alive, panel, out_blocks, pattern):
    tiles = panel.astype(jnp.float32).reshape(-1, BLK, RANK)

    def visit(total, item):
        block_values, take_row, place_row, alive_row = item
        picked = tiles[take_row]
        products = jnp.einsum(pattern, block_values.astype(jnp.float32), picked, precision=highest)
        products = jnp.where(alive_row[:, None, None], products, jnp.float32(0.0))
        return (total.at[place_row].add(products), None)
    empty = jnp.zeros((out_blocks, BLK, RANK), jnp.float32)
    total, _ = lax.scan(visit, empty, (values, take_ids, place_ids, alive))
    return total.reshape(out_blocks * BLK, RANK)

def orthonormal(matrix, total_rows):
    gram_sum = jnp.dot(matrix.T.astype(jnp.float32), matrix.astype(jnp.float32), precision=highest, preferred_element_type=jnp.float32)
    factor = jnp.linalg.cholesky(gram_sum / total_rows)
    return lax.linalg.triangular_solve(factor, matrix, left_side=False, lower=True, transpose_a=True)

def reference(values, block_rows, block_cols, block_count, test_matrix):
    prefix_ids, suffix_ids = block_places(block_rows, block_cols)
    alive = jnp.arange(CAP, dtype=jnp.int32)[None, :] < block_count[:, None]
    sketch = block_product(values, suffix_ids, prefix_ids, alive, test_matrix, PRE_BLOCKS, 'gij,gjr->gir')
    first_basis = orthonormal(sketch, PREFIXES)
    first_rounded = lax.optimization_barrier(first_basis.astype(jnp.bfloat16))
    suffix_raw = block_product(values, prefix_ids, suffix_ids, alive, first_rounded, SUF_BLOCKS, 'gji,gjr->gir')
    suffix_basis = orthonormal(suffix_raw, SUFFIXES)
    suffix_rounded = lax.optimization_barrier(suffix_basis.astype(jnp.bfloat16))
    refined = block_product(values, suffix_ids, prefix_ids, alive, suffix_rounded, PRE_BLOCKS, 'gij,gjr->gir')
    prefix_basis = orthonormal(refined, PREFIXES)
    return (prefix_basis, suffix_basis)
```

```python
import functools

import jax
import jax.numpy as jnp
from jax import lax
from jax.experimental import pallas as pl
from jax.experimental.pallas import tpu as pltpu
from jax.sharding import PartitionSpec as P

BLK = 128
PB = 16
SB = 16
TILE = 128
SUB = 8
RING = 4
VMEM_BYTES = 48 * 1024 * 1024

highest = lax.Precision.HIGHEST


def dense_kernel(count_ref, rows_ref, cols_ref, values_ref, out_ref, sem):
    out_ref[...] = jnp.zeros(out_ref.shape, out_ref.dtype)
    live = count_ref[0]

    def copy(k):
        row = pl.multiple_of(rows_ref[k] * BLK, BLK)
        col = pl.multiple_of(cols_ref[k] * BLK, BLK)
        return pltpu.make_async_copy(
            values_ref.at[k], out_ref.at[pl.ds(row, BLK), pl.ds(col, BLK)], sem
        )

    def start(k, carry):
        copy(k).start()
        return carry

    def wait(k, carry):
        copy(k).wait()
        return carry

    lax.fori_loop(0, live, start, 0)
    lax.fori_loop(0, live, wait, 0)


def dense_blocks(block_values, row_ids, col_ids, live_count):
    smem = pl.BlockSpec(memory_space=pltpu.SMEM)
    return pl.pallas_call(
        dense_kernel,
        out_shape=jax.ShapeDtypeStruct((PB * BLK, SB * BLK), jnp.bfloat16),
        in_specs=[smem, smem, smem, pl.BlockSpec(memory_space=pl.ANY)],
        out_specs=pl.BlockSpec(memory_space=pltpu.VMEM),
        scratch_shapes=[pltpu.SemaphoreType.DMA],
        compiler_params=pltpu.CompilerParams(vmem_limit_bytes=VMEM_BYTES),
        name="dense_blocks",
    )(live_count, row_ids, col_ids, block_values)


def orth_kernel(gram_ref, rows_ref, *refs, scale, rounded):
    if rounded:
        round_ref, out_ref, work_ref, panel_ref, spread_ref = refs
    else:
        out_ref, work_ref, panel_ref, spread_ref = refs
    rank = gram_ref.shape[0]
    panels = rank // TILE
    groups = TILE // SUB
    work_ref[...] = gram_ref[...] * scale
    for p in range(panels):
        width = rank - p * TILE
        total = width + TILE
        panel_ref[:, :width] = work_ref[p * TILE:(p + 1) * TILE, p * TILE:]
        row_ids = lax.broadcasted_iota(jnp.int32, (TILE, TILE), 0)
        lane_ids = lax.broadcasted_iota(jnp.int32, (TILE, TILE), 1)
        panel_ref[:, width:total] = jnp.where(row_ids == lane_ids, 1.0, 0.0).astype(jnp.float32)

        def step(b, first_group, total=total):
            base = pl.multiple_of(b * SUB, SUB)
            shift = (TILE - base) % TILE
            square = pltpu.roll(panel_ref[pl.ds(base, SUB), :TILE], shift, 1)
            for j in range(SUB):
                spread_ref[j] = jnp.broadcast_to(square[:, j:j + 1], (SUB, TILE))
            e = [
                [jnp.broadcast_to(spread_ref[j, i:i + 1, :], (SUB, TILE)) for j in range(i + 1)]
                for i in range(SUB)
            ]
            inv = [None] * SUB
            for k in range(SUB):
                inv[k] = lax.rsqrt(e[k][k])
                for i in range(k + 1, SUB):
                    e[i][k] = e[i][k] * inv[k]
                for i in range(k + 1, SUB):
                    for j in range(k + 1, i + 1):
                        e[i][j] = e[i][j] - e[i][k] * e[j][k]
            tiles = total // TILE
            strip = [panel_ref[pl.ds(base, SUB), t * TILE:(t + 1) * TILE] for t in range(tiles)]
            r = []
            for k in range(SUB):
                row = []
                for t in range(tiles):
                    v = jnp.broadcast_to(strip[t][k:k + 1, :], (SUB, TILE))
                    for j in range(k):
                        v = v - e[k][j] * r[j][t]
                    row.append(v * inv[k])
                r.append(row)
            sub_ids = lax.broadcasted_iota(jnp.int32, (SUB, TILE), 0)
            for t in range(tiles):
                v = r[0][t]
                for k in range(1, SUB):
                    v = jnp.where(sub_ids == k, r[k][t], v)
                panel_ref[pl.ds(base, SUB), t * TILE:(t + 1) * TILE] = v
                if t == 0:
                    turned = v.T
            for g in range(first_group, groups):
                lo = g * SUB
                mult = jnp.where(g > b, turned[lo:lo + SUB, :], 0.0)
                cols = [jnp.broadcast_to(mult[:, k:k + 1], (SUB, TILE)) for k in range(SUB)]
                for t in range(tiles):
                    v = panel_ref[lo:lo + SUB, t * TILE:(t + 1) * TILE]
                    for k in range(SUB):
                        v = v - cols[k] * r[k][t]
                    panel_ref[lo:lo + SUB, t * TILE:(t + 1) * TILE] = v

        parts = 4
        for q in range(parts):
            size = groups // parts

            def body(i, carry, q=q, size=size, step=step):
                step(q * size + i, q * size + 1)
                return carry

            lax.fori_loop(0, size, body, 0)

        for q in range(p + 1, panels):
            lhs = panel_ref[:, (q - p) * TILE:(q - p + 1) * TILE]
            rhs = panel_ref[:, (q - p) * TILE:width]
            update = lax.dot_general(
                lhs, rhs, (((0,), (0,)), ((), ())), precision=highest,
                preferred_element_type=jnp.float32,
            )
            work_ref[q * TILE:(q + 1) * TILE, q * TILE:] = (
                work_ref[q * TILE:(q + 1) * TILE, q * TILE:] - update
            )
        left = rows_ref[:, p * TILE:(p + 1) * TILE]
        for q in range(p):
            left = left - jnp.dot(
                out_ref[:, q * TILE:(q + 1) * TILE],
                work_ref[q * TILE:(q + 1) * TILE, p * TILE:(p + 1) * TILE],
                precision=highest, preferred_element_type=jnp.float32,
            )
        solved = lax.dot_general(
            left, panel_ref[:, width:total], (((1,), (1,)), ((), ())), precision=highest,
            preferred_element_type=jnp.float32,
        )
        out_ref[:, p * TILE:(p + 1) * TILE] = solved
        if rounded:
            round_ref[:, p * TILE:(p + 1) * TILE] = solved.astype(jnp.bfloat16)
        work_ref[p * TILE:(p + 1) * TILE, p * TILE:] = panel_ref[:, :width]


def orthonormal(matrix, gram, total_rows, rounded):
    rank = gram.shape[0]
    wide = jax.ShapeDtypeStruct(matrix.shape, jnp.float32)
    narrow = jax.ShapeDtypeStruct(matrix.shape, jnp.bfloat16)
    return pl.pallas_call(
        functools.partial(orth_kernel, scale=1.0 / total_rows, rounded=rounded),
        out_shape=(narrow, wide) if rounded else wide,
        scratch_shapes=[
            pltpu.VMEM((rank, rank), jnp.float32),
            pltpu.VMEM((TILE, rank + TILE), jnp.float32),
            pltpu.VMEM((SUB, SUB, TILE), jnp.float32),
        ],
        compiler_params=pltpu.CompilerParams(vmem_limit_bytes=VMEM_BYTES),
        name="orth",
    )(gram, matrix)


def along(axis, step):
    pairs = []
    for y in range(RING):
        for x in range(RING):
            for core in range(2):
                to = {
                    "y": ((y + step) % RING, x, core),
                    "x": (y, (x + step) % RING, core),
                    "core": (y, x, 1 - core),
                }[axis]
                pairs.append(((y * RING + x) * 2 + core, (to[0] * RING + to[1]) * 2 + to[2]))
    return pairs


def to_suf(value, step):
    return lax.ppermute(value, "suf", [(s, (s + step) % RING) for s in range(RING)])


def to_pre(value, axis, step=1):
    return lax.ppermute(value, "pre", along(axis, step))


def gather_suf(value):
    return jnp.concatenate([value] + [to_suf(value, -k) for k in range(1, RING)], axis=0)


def gather_pre(value, core):
    held = value[None]
    for axis in ("y", "x"):
        held = jnp.stack([held] + [to_pre(held, axis, -k) for k in range(1, RING)], axis=0)
    held = jnp.swapaxes(held[:, :, 0], 0, 1)
    other = to_pre(held, "core")
    first = jnp.where(core == 0, held, other)
    second = jnp.where(core == 0, other, held)
    full = jnp.stack([first, second], axis=2)
    return full.reshape(-1, value.shape[-1])


def scatter_suf(chunks):
    total = chunks[0]
    for k in (2, 1, 3):
        total = total + to_suf(chunks[k], k)
    return total


def scatter_pre(partial_value, core):
    rows, columns = partial_value.shape
    held = partial_value.reshape(RING, RING, 2, rows // (RING * RING * 2), columns)
    mine = jnp.where(core == 0, held[:, :, 0], held[:, :, 1])
    theirs = jnp.where(core == 0, held[:, :, 1], held[:, :, 0])
    held = mine + to_pre(theirs, "core")
    for axis in ("y", "x"):
        total = held[0]
        for k in range(1, RING):
            total = total + to_pre(held[k], axis, k)
        held = total
    return held


def sum_all(gram):
    rank = gram.shape[0]
    pre = lax.axis_size("pre")
    pieces = lax.all_to_all(gram, "pre", 0, 0, tiled=True)
    piece = jnp.sum(pieces.reshape(pre, rank // pre, rank), axis=0)
    total = piece
    for k in range(1, RING):
        total = total + to_suf(piece, k)
    spread = jnp.broadcast_to(total[None], (pre,) + total.shape)
    return lax.all_to_all(spread, "pre", 0, 0, tiled=True).reshape(rank, rank)


def gram_of(matrix):
    return jnp.dot(matrix.T, matrix, precision=highest, preferred_element_type=jnp.float32)


def local(values, block_rows, block_cols, block_count, test_matrix):
    pre, suf = lax.axis_index("pre"), lax.axis_index("suf")
    core, x, y = pre % 2, pre // 2 % RING, pre // (2 * RING)
    prefix_total = PB * BLK * lax.axis_size("pre")
    suffix_total = SB * BLK * lax.axis_size("suf")
    row_ids = ((block_rows[0] // RING - suf) % RING) * RING + block_rows[0] % RING
    col_ids = ((block_cols[0] // RING - y) % RING) * RING + (block_cols[0] % RING - x) % RING
    panel = gather_pre(test_matrix, core)
    dense = dense_blocks(values[0], row_ids, col_ids, block_count)
    share_rows = PB * BLK // RING

    def prefix_sums(panel):
        chunks = [None] * RING
        for k in (2, 1, 3, 0):
            chunks[k] = jnp.dot(
                dense[k * share_rows:(k + 1) * share_rows], panel,
                preferred_element_type=jnp.float32,
            )
        return scatter_suf(chunks)

    sketch = prefix_sums(panel)
    first_rounded, _ = orthonormal(sketch, sum_all(gram_of(sketch)), prefix_total, True)
    suffix_partial = lax.dot_general(
        dense, gather_suf(first_rounded), (((0,), (0,)), ((), ())),
        preferred_element_type=jnp.float32,
    )
    suffix_raw = scatter_pre(suffix_partial, core)
    suffix_rounded, suffix_basis = orthonormal(
        suffix_raw, sum_all(gram_of(suffix_raw)), suffix_total, True
    )
    refined = prefix_sums(gather_pre(suffix_rounded, core))
    prefix_basis = orthonormal(refined, sum_all(gram_of(refined)), prefix_total, False)
    return (prefix_basis, suffix_basis)


def solution(mesh):
    in_specs = (
        P(("pre", "suf"), None, None, None),
        P(("pre", "suf"), None),
        P(("pre", "suf"), None),
        P(("pre", "suf")),
        P(("suf", "pre"), None),
    )
    out_specs = (P(("pre", "suf"), None), P(("suf", "pre"), None))
    return jax.shard_map(local, mesh=mesh, in_specs=in_specs, out_specs=out_specs, check_vma=False)
```

```python
import functools

import jax
import jax.numpy as jnp
from jax import lax
from jax.experimental import pallas as pl
from jax.experimental.pallas import tpu as pltpu
from jax.sharding import PartitionSpec as P

BLK = 128
PB = 16
SB = 16
TILE = 128
SUB = 8
RING = 4
VMEM_BYTES = 48 * 1024 * 1024

highest = lax.Precision.HIGHEST


def dense_kernel(count_ref, rows_ref, cols_ref, values_ref, out_ref, sem):
    out_ref[...] = jnp.zeros(out_ref.shape, out_ref.dtype)
    live = count_ref[0]

    def copy(k):
        row = pl.multiple_of(rows_ref[k] * BLK, BLK)
        col = pl.multiple_of(cols_ref[k] * BLK, BLK)
        return pltpu.make_async_copy(
            values_ref.at[k], out_ref.at[pl.ds(row, BLK), pl.ds(col, BLK)], sem
        )

    def start(k, carry):
        copy(k).start()
        return carry

    def wait(k, carry):
        copy(k).wait()
        return carry

    lax.fori_loop(0, live, start, 0)
    lax.fori_loop(0, live, wait, 0)


def dense_blocks(block_values, row_ids, col_ids, live_count):
    smem = pl.BlockSpec(memory_space=pltpu.SMEM)
    return pl.pallas_call(
        dense_kernel,
        out_shape=jax.ShapeDtypeStruct((PB * BLK, SB * BLK), jnp.bfloat16),
        in_specs=[smem, smem, smem, pl.BlockSpec(memory_space=pl.ANY)],
        out_specs=pl.BlockSpec(memory_space=pltpu.VMEM),
        scratch_shapes=[pltpu.SemaphoreType.DMA],
        compiler_params=pltpu.CompilerParams(vmem_limit_bytes=VMEM_BYTES),
        name="dense_blocks",
    )(live_count, row_ids, col_ids, block_values)


def tile_pairs(rank):
    panels = rank // TILE
    return [(p, t) for p in range(panels) for t in range(p, panels)]


def gram_kernel(*refs):
    parts, (total_ref, gram_ref) = refs[:-2], refs[-2:]
    total = parts[0][...]
    for part in parts[1:]:
        total = total + part[...]
    total_ref[...] = total
    rank = total.shape[1]
    at = 0
    for p in range(rank // TILE):
        row = lax.dot_general(
            total[:, p * TILE:(p + 1) * TILE], total[:, p * TILE:], (((0,), (0,)), ((), ())),
            precision=highest, preferred_element_type=jnp.float32,
        )
        for t in range(rank // TILE - p):
            gram_ref[at:at + TILE, :] = row[:, t * TILE:(t + 1) * TILE]
            at += TILE


def sum_and_gram(parts):
    rows, rank = parts[0].shape
    packed = len(tile_pairs(rank)) * TILE
    return pl.pallas_call(
        gram_kernel,
        out_shape=(
            jax.ShapeDtypeStruct((rows, rank), jnp.float32),
            jax.ShapeDtypeStruct((packed, TILE), jnp.float32),
        ),
        compiler_params=pltpu.CompilerParams(vmem_limit_bytes=VMEM_BYTES),
        name="gram",
    )(*parts)


def eliminate(panel_ref, spread_ref):
    total = panel_ref.shape[1]
    tiles = total // TILE
    groups = TILE // SUB
    sub_ids = lax.broadcasted_iota(jnp.int32, (SUB, TILE), 0)
    for b in range(groups):
        base = b * SUB
        here = slice(base, base + SUB)
        square = panel_ref[here, here]
        slot = b % 2
        for j in range(SUB):
            spread_ref[slot, j] = jnp.broadcast_to(square[:, j:j + 1], (SUB, TILE))
        e = [
            [jnp.broadcast_to(spread_ref[slot, j, i:i + 1, :], (SUB, TILE)) for j in range(i + 1)]
            for i in range(SUB)
        ]
        if b + 1 < groups:
            below = panel_ref[base + SUB:base + 2 * SUB, here]
            raw = [jnp.broadcast_to(below[:, k:k + 1], (SUB, TILE)) for k in range(SUB)]
        inv = [None] * SUB
        for k in range(SUB):
            inv[k] = lax.rsqrt(e[k][k])
            for i in range(k + 1, SUB):
                e[i][k] = e[i][k] * inv[k]
            for i in range(k + 1, SUB):
                for j in range(k + 1, i + 1):
                    e[i][j] = e[i][j] - e[i][k] * e[j][k]
        r = []
        for k in range(SUB):
            row = []
            for t in range(tiles):
                v = jnp.broadcast_to(panel_ref[base + k:base + k + 1, t * TILE:(t + 1) * TILE], (SUB, TILE))
                for j in range(k):
                    v = v - e[k][j] * r[j][t]
                row.append(v * inv[k])
            r.append(row)
        for t in range(tiles):
            v = r[0][t]
            for k in range(1, SUB):
                v = jnp.where(sub_ids == k, r[k][t], v)
            panel_ref[here, t * TILE:(t + 1) * TILE] = v
            if t == 0:
                turned = v.T
        for g in range(b + 1, groups):
            there = slice(g * SUB, (g + 1) * SUB)
            if g == b + 1:
                cols = []
                for k in range(SUB):
                    v = raw[k]
                    for j in range(k):
                        v = v - e[k][j] * cols[j]
                    cols.append(v * inv[k])
            else:
                cols = [jnp.broadcast_to(turned[there, k:k + 1], (SUB, TILE)) for k in range(SUB)]
            for t in range(tiles):
                v = panel_ref[there, t * TILE:(t + 1) * TILE]
                for k in range(SUB):
                    v = v - cols[k] * r[k][t]
                panel_ref[there, t * TILE:(t + 1) * TILE] = v


def orth_kernel(gram_ref, rows_ref, *refs, scale, rounded):
    if rounded:
        round_ref, out_ref, work_ref, left_ref, panel_ref, spread_ref = refs
    else:
        out_ref, work_ref, left_ref, panel_ref, spread_ref = refs
    rank = rows_ref.shape[1]
    panels = rank // TILE
    pairs = tile_pairs(rank)
    for t in range(panels):
        for p in range(panels):
            rows = slice(p * TILE, (p + 1) * TILE)
            if (p, t) in pairs:
                at = pairs.index((p, t)) * TILE
                work_ref[t, rows, :] = gram_ref[at:at + TILE, :] * scale
            else:
                work_ref[t, rows, :] = jnp.zeros((TILE, TILE), jnp.float32)
        left_ref[t] = rows_ref[:, t * TILE:(t + 1) * TILE]
    row_ids = lax.broadcasted_iota(jnp.int32, (TILE, TILE), 0)
    lane_ids = lax.broadcasted_iota(jnp.int32, (TILE, TILE), 1)
    unit = jnp.where(row_ids == lane_ids, 1.0, 0.0).astype(jnp.float32)

    def panel_step(p, carry):
        rows = pl.ds(pl.multiple_of(p * TILE, TILE), TILE)
        for t in range(panels):
            panel_ref[:, t * TILE:(t + 1) * TILE] = work_ref[(p + t) % panels, rows, :]
        panel_ref[:, rank:rank + TILE] = unit
        eliminate(panel_ref, spread_ref)
        solved = lax.dot_general(
            left_ref[p], panel_ref[:, rank:rank + TILE], (((1,), (1,)), ((), ())), precision=highest,
            preferred_element_type=jnp.float32,
        )
        for t in range(panels):
            @pl.when(p == t)
            def _():
                out_ref[:, t * TILE:(t + 1) * TILE] = solved
                if rounded:
                    round_ref[:, t * TILE:(t + 1) * TILE] = solved.astype(jnp.bfloat16)
        @pl.when(p < panels - 1)
        def _():
            across = panel_ref[:, TILE:rank]
            moved = jnp.dot(solved, across, precision=highest, preferred_element_type=jnp.float32)
            update = lax.dot_general(
                across, across, (((0,), (0,)), ((), ())), precision=highest,
                preferred_element_type=jnp.float32,
            )
            for t in range(1, panels):
                tile = (p + t) % panels
                lanes = slice((t - 1) * TILE, t * TILE)
                left_ref[tile] = left_ref[tile] - moved[:, lanes]
                for u in range(1, panels):
                    under = pl.ds(pl.multiple_of((p + u) % panels * TILE, TILE), TILE)
                    work_ref[tile, under, :] = (
                        work_ref[tile, under, :] - update[(u - 1) * TILE:u * TILE, lanes]
                    )
        return carry

    lax.fori_loop(0, panels, panel_step, 0)


def orthonormal(matrix, gram, total_rows, rounded):
    rank = matrix.shape[1]
    wide = jax.ShapeDtypeStruct(matrix.shape, jnp.float32)
    narrow = jax.ShapeDtypeStruct(matrix.shape, jnp.bfloat16)
    return pl.pallas_call(
        functools.partial(orth_kernel, scale=1.0 / total_rows, rounded=rounded),
        out_shape=(narrow, wide) if rounded else wide,
        scratch_shapes=[
            pltpu.VMEM((rank // TILE, rank, TILE), jnp.float32),
            pltpu.VMEM((rank // TILE, matrix.shape[0], TILE), jnp.float32),
            pltpu.VMEM((TILE, rank + TILE), jnp.float32),
            pltpu.VMEM((2, SUB, SUB, TILE), jnp.float32),
        ],
        compiler_params=pltpu.CompilerParams(vmem_limit_bytes=VMEM_BYTES),
        name="orth",
    )(gram, matrix)


def along(axis, step):
    pairs = []
    for y in range(RING):
        for x in range(RING):
            for core in range(2):
                to = {
                    "y": ((y + step) % RING, x, core),
                    "x": (y, (x + step) % RING, core),
                    "core": (y, x, 1 - core),
                }[axis]
                pairs.append(((y * RING + x) * 2 + core, (to[0] * RING + to[1]) * 2 + to[2]))
    return pairs


def to_suf(value, step):
    return lax.ppermute(value, "suf", [(s, (s + step) % RING) for s in range(RING)])


def to_pre(value, axis, step=1):
    return lax.ppermute(value, "pre", along(axis, step))


def gather_suf(value):
    return jnp.concatenate([value] + [to_suf(value, -k) for k in range(1, RING)], axis=0)


def gather_pre(value, core, beside=None):
    held = value[None]
    for axis in ("y", "x"):
        held = jnp.stack([held] + [to_pre(held, axis, -k) for k in range(1, RING)], axis=0)
    held = jnp.swapaxes(held[:, :, 0], 0, 1)
    if beside is not None:
        held, beside = lax.optimization_barrier((held, beside))
    other = to_pre(held, "core")
    first = jnp.where(core == 0, held, other)
    second = jnp.where(core == 0, other, held)
    full = jnp.stack([first, second], axis=2)
    full = full.reshape(-1, value.shape[-1])
    return full if beside is None else (full, beside)


def scatter_suf(chunks):
    moved = {k: to_suf(chunks[k], k) for k in (2, 1, 3)}
    return [chunks[0]] + [moved[k] for k in (1, 2, 3)]


def scatter_pre(partial_value, core):
    rows, columns = partial_value.shape
    share = rows // (RING * RING * 2)
    held = partial_value.reshape(RING, RING, 2, share, columns)
    mine = jnp.where(core == 0, held[:, :, 0], held[:, :, 1])
    theirs = jnp.where(core == 0, held[:, :, 1], held[:, :, 0])
    held = mine + to_pre(theirs, "core")
    upper, lower = held[:, :, :share // 2], held[:, :, share // 2:]
    upper_parts = [upper[k] if k == 0 else to_pre(upper[k], "y", k) for k in range(RING)]
    lower_parts = [lower[:, k] if k == 0 else to_pre(lower[:, k], "x", k) for k in range(RING)]
    upper, lower = sum(upper_parts[1:], upper_parts[0]), sum(lower_parts[1:], lower_parts[0])
    upper_parts = [upper[k] if k == 0 else to_pre(upper[k], "x", k) for k in range(RING)]
    lower_parts = [lower[k] if k == 0 else to_pre(lower[k], "y", k) for k in range(RING)]
    return [jnp.concatenate(pair, axis=0) for pair in zip(upper_parts, lower_parts)]


def swap_chips(value):
    groups = [[chip * 2 + core for chip in range(RING * RING)] for core in range(2)]
    return lax.all_to_all(value, "pre", 0, 0, axis_index_groups=groups, tiled=True)


def sum_all(gram, core):
    rows, lanes = gram.shape
    chips = RING * RING
    half = rows // 2
    low, high = gram[:half], gram[half:]
    mine = jnp.where(core == 0, low, high)
    mine = mine + to_pre(jnp.where(core == 0, high, low), "core")
    pieces = swap_chips(mine)
    piece = jnp.sum(pieces.reshape(chips, half // chips, lanes), axis=0)
    parts = [piece] + [to_suf(piece, k) for k in range(1, RING)]
    total = sum(parts[1:], parts[0])
    spread = jnp.broadcast_to(total[None], (chips,) + total.shape).reshape(half, lanes)
    mine = swap_chips(spread)
    other = to_pre(mine, "core")
    low = jnp.where(core == 0, mine, other)
    high = jnp.where(core == 0, other, mine)
    return jnp.concatenate([low, high], axis=0)


def local(values, block_rows, block_cols, block_count, test_matrix):
    pre, suf = lax.axis_index("pre"), lax.axis_index("suf")
    core, x, y = pre % 2, pre // 2 % RING, pre // (2 * RING)
    prefix_total = PB * BLK * lax.axis_size("pre")
    suffix_total = SB * BLK * lax.axis_size("suf")
    row_ids = ((block_rows[0] // RING - suf) % RING) * RING + block_rows[0] % RING
    col_ids = ((block_cols[0] // RING - y) % RING) * RING + (block_cols[0] % RING - x) % RING
    dense = dense_blocks(values[0], row_ids, col_ids, block_count)
    panel, dense = gather_pre(test_matrix, core, dense)
    share_rows = PB * BLK // RING

    def prefix_sums(panel):
        chunks = [None] * RING
        for k in (2, 1, 3, 0):
            chunks[k] = jnp.dot(
                dense[k * share_rows:(k + 1) * share_rows], panel,
                preferred_element_type=jnp.float32,
            )
        return sum_and_gram(scatter_suf(chunks))

    sketch, gram = prefix_sums(panel)
    first_rounded, _ = orthonormal(sketch, sum_all(gram, core), prefix_total, True)
    suffix_partial = lax.dot_general(
        dense, gather_suf(first_rounded), (((0,), (0,)), ((), ())),
        preferred_element_type=jnp.float32,
    )
    suffix_raw, gram = sum_and_gram(scatter_pre(suffix_partial, core))
    suffix_rounded, suffix_basis = orthonormal(
        suffix_raw, sum_all(gram, core), suffix_total, True
    )
    refined, gram = prefix_sums(gather_pre(suffix_rounded, core))
    prefix_basis = orthonormal(refined, sum_all(gram, core), prefix_total, False)
    return (prefix_basis, suffix_basis)


def solution(mesh):
    in_specs = (
        P(("pre", "suf"), None, None, None),
        P(("pre", "suf"), None),
        P(("pre", "suf"), None),
        P(("pre", "suf")),
        P(("suf", "pre"), None),
    )
    out_specs = (P(("pre", "suf"), None), P(("suf", "pre"), None))
    return jax.shard_map(local, mesh=mesh, in_specs=in_specs, out_specs=out_specs, check_vma=False)
```

```python
import functools

import jax
import jax.numpy as jnp
from jax import lax
from jax.experimental import pallas as pl
from jax.experimental.pallas import tpu as pltpu
from jax.sharding import PartitionSpec as P

BLK = 128
PB = 16
SB = 16
TILE = 128
SUB = 8
RING = 4
VMEM_BYTES = 48 * 1024 * 1024

highest = lax.Precision.HIGHEST


def dense_kernel(count_ref, rows_ref, cols_ref, values_ref, out_ref, sem):
    out_ref[...] = jnp.zeros(out_ref.shape, out_ref.dtype)
    live = count_ref[0]

    def copy(k):
        row = pl.multiple_of(rows_ref[k] * BLK, BLK)
        col = pl.multiple_of(cols_ref[k] * BLK, BLK)
        return pltpu.make_async_copy(
            values_ref.at[k], out_ref.at[pl.ds(row, BLK), pl.ds(col, BLK)], sem
        )

    def start(k, carry):
        copy(k).start()
        return carry

    def wait(k, carry):
        copy(k).wait()
        return carry

    lax.fori_loop(0, live, start, 0)
    lax.fori_loop(0, live, wait, 0)


def dense_blocks(block_values, row_ids, col_ids, live_count):
    smem = pl.BlockSpec(memory_space=pltpu.SMEM)
    return pl.pallas_call(
        dense_kernel,
        out_shape=jax.ShapeDtypeStruct((PB * BLK, SB * BLK), jnp.bfloat16),
        in_specs=[smem, smem, smem, pl.BlockSpec(memory_space=pl.ANY)],
        out_specs=pl.BlockSpec(memory_space=pltpu.VMEM),
        scratch_shapes=[pltpu.SemaphoreType.DMA],
        compiler_params=pltpu.CompilerParams(vmem_limit_bytes=VMEM_BYTES),
        name="dense_blocks",
    )(live_count, row_ids, col_ids, block_values)


def tile_pairs(rank):
    panels = rank // TILE
    return [(p, t) for p in range(panels) for t in range(p, panels)]


def gram_kernel(*refs, count):
    parts, (left_ref, right_ref, gram_ref) = refs[:-3], refs[-3:]
    rows, half = left_ref.shape
    whole = len(parts) == count
    for total_ref, mine, lane in (
        (left_ref, parts[:count], 0), (right_ref, parts if whole else parts[count:], half if whole else 0)
    ):
        total = None
        for part in mine:
            for at in range(0, part.shape[0], rows):
                chunk = part[at:at + rows, lane:lane + half]
                total = chunk if total is None else total + chunk
        total_ref[...] = total
    total = jnp.concatenate([left_ref[...], right_ref[...]], axis=1)
    rank = 2 * half
    at = 0
    for p in range(rank // TILE):
        row = lax.dot_general(
            total[:, p * TILE:(p + 1) * TILE], total[:, p * TILE:], (((0,), (0,)), ((), ())),
            precision=highest, preferred_element_type=jnp.float32,
        )
        for t in range(rank // TILE - p):
            gram_ref[at:at + TILE, :] = row[:, t * TILE:(t + 1) * TILE]
            at += TILE


def sum_and_gram(left_parts, right_parts, rows):
    half = left_parts[0].shape[1] // (1 if right_parts else 2)
    packed = len(tile_pairs(2 * half)) * TILE
    share = jax.ShapeDtypeStruct((rows, half), jnp.float32)
    return pl.pallas_call(
        functools.partial(gram_kernel, count=len(left_parts)),
        out_shape=(share, share, jax.ShapeDtypeStruct((packed, TILE), jnp.float32)),
        compiler_params=pltpu.CompilerParams(vmem_limit_bytes=VMEM_BYTES),
        name="gram",
    )(*left_parts, *right_parts)


def eliminate(panel_ref, spread_ref):
    total = panel_ref.shape[1]
    tiles = total // TILE
    groups = TILE // SUB
    sub_ids = lax.broadcasted_iota(jnp.int32, (SUB, TILE), 0)
    for b in range(groups):
        base = b * SUB
        here = slice(base, base + SUB)
        square = panel_ref[here, here]
        slot = b % 2
        for j in range(SUB):
            spread_ref[slot, j] = jnp.broadcast_to(square[:, j:j + 1], (SUB, TILE))
        e = [
            [jnp.broadcast_to(spread_ref[slot, j, i:i + 1, :], (SUB, TILE)) for j in range(i + 1)]
            for i in range(SUB)
        ]
        if b + 1 < groups:
            below = panel_ref[base + SUB:base + 2 * SUB, here]
            raw = [jnp.broadcast_to(below[:, k:k + 1], (SUB, TILE)) for k in range(SUB)]
        inv = [None] * SUB
        for k in range(SUB):
            inv[k] = lax.rsqrt(e[k][k])
            for i in range(k + 1, SUB):
                e[i][k] = e[i][k] * inv[k]
            for i in range(k + 1, SUB):
                for j in range(k + 1, i + 1):
                    e[i][j] = e[i][j] - e[i][k] * e[j][k]
        r = []
        for k in range(SUB):
            row = []
            for t in range(tiles):
                v = jnp.broadcast_to(panel_ref[base + k:base + k + 1, t * TILE:(t + 1) * TILE], (SUB, TILE))
                for j in range(k):
                    v = v - e[k][j] * r[j][t]
                row.append(v * inv[k])
            r.append(row)
        for t in range(tiles):
            v = r[0][t]
            for k in range(1, SUB):
                v = jnp.where(sub_ids == k, r[k][t], v)
            panel_ref[here, t * TILE:(t + 1) * TILE] = v
            if t == 0:
                turned = v.T
        for g in range(b + 1, groups):
            there = slice(g * SUB, (g + 1) * SUB)
            if g == b + 1:
                cols = []
                for k in range(SUB):
                    v = raw[k]
                    for j in range(k):
                        v = v - e[k][j] * cols[j]
                    cols.append(v * inv[k])
            else:
                cols = [jnp.broadcast_to(turned[there, k:k + 1], (SUB, TILE)) for k in range(SUB)]
            for t in range(tiles):
                v = panel_ref[there, t * TILE:(t + 1) * TILE]
                for k in range(SUB):
                    v = v - cols[k] * r[k][t]
                panel_ref[there, t * TILE:(t + 1) * TILE] = v


def factor_and_solve(work_ref, left_ref, panel_ref, spread_ref, store):
    panels = work_ref.shape[0]
    rank = panels * TILE
    row_ids = lax.broadcasted_iota(jnp.int32, (TILE, TILE), 0)
    lane_ids = lax.broadcasted_iota(jnp.int32, (TILE, TILE), 1)
    unit = jnp.where(row_ids == lane_ids, 1.0, 0.0).astype(jnp.float32)

    def panel_step(p, carry):
        rows = pl.ds(pl.multiple_of(p * TILE, TILE), TILE)
        for t in range(panels):
            panel_ref[:, t * TILE:(t + 1) * TILE] = work_ref[(p + t) % panels, rows, :]
        panel_ref[:, rank:rank + TILE] = unit
        eliminate(panel_ref, spread_ref)
        solved = lax.dot_general(
            left_ref[p], panel_ref[:, rank:rank + TILE], (((1,), (1,)), ((), ())), precision=highest,
            preferred_element_type=jnp.float32,
        )
        for t in range(panels):
            @pl.when(p == t)
            def _():
                store(t, solved)

        @pl.when(p < panels - 1)
        def _():
            across = panel_ref[:, TILE:rank]
            moved = jnp.dot(solved, across, precision=highest, preferred_element_type=jnp.float32)
            update = lax.dot_general(
                across, across, (((0,), (0,)), ((), ())), precision=highest,
                preferred_element_type=jnp.float32,
            )
            for t in range(1, panels):
                tile = (p + t) % panels
                lanes = slice((t - 1) * TILE, t * TILE)
                left_ref[tile] = left_ref[tile] - moved[:, lanes]
                for u in range(1, panels):
                    under = pl.ds(pl.multiple_of((p + u) % panels * TILE, TILE), TILE)
                    work_ref[tile, under, :] = (
                        work_ref[tile, under, :] - update[(u - 1) * TILE:u * TILE, lanes]
                    )
        return carry

    lax.fori_loop(0, panels, panel_step, 0)


def tile_of(gram_ref, rank, p, t, scale):
    at = tile_pairs(rank).index((p, t)) * TILE
    return gram_ref[at:at + TILE, :] * scale


def left_kernel(gram_ref, rows_ref, *refs, scale, rounded):
    if rounded:
        round_ref, out_ref, factor_ref, work_ref, left_ref, panel_ref, spread_ref = refs
    else:
        out_ref, factor_ref, work_ref, left_ref, panel_ref, spread_ref = refs
    half = rows_ref.shape[1]
    panels = half // TILE
    for t in range(panels):
        lanes = slice(t * TILE, (t + 1) * TILE)
        for p in range(panels):
            rows = slice(p * TILE, (p + 1) * TILE)
            if p <= t:
                work_ref[t, rows, :] = tile_of(gram_ref, 2 * half, p, t, scale)
            else:
                work_ref[t, rows, :] = jnp.zeros((TILE, TILE), jnp.float32)
        left_ref[t] = rows_ref[:, lanes]

    def store(t, solved):
        lanes = slice(t * TILE, (t + 1) * TILE)
        out_ref[:, lanes] = solved
        if rounded:
            round_ref[:, lanes] = solved.astype(jnp.bfloat16)
        factor_ref[t] = panel_ref[...]

    factor_and_solve(work_ref, left_ref, panel_ref, spread_ref, store)


def right_kernel(gram_ref, rows_ref, first_ref, factor_ref, *refs, scale, rounded):
    if rounded:
        round_ref, out_ref, work_ref, left_ref, panel_ref, spread_ref = refs
    else:
        out_ref, work_ref, left_ref, panel_ref, spread_ref = refs
    half = rows_ref.shape[1]
    panels = half // TILE
    rank = 2 * half

    def dot(a, b, dims):
        return lax.dot_general(
            a, b, ((dims[:1], dims[1:]), ((), ())), precision=highest,
            preferred_element_type=jnp.float32,
        )

    above = []
    for p in range(panels):
        g = jnp.concatenate(
            [tile_of(gram_ref, rank, p, panels + t, scale) for t in range(panels)], axis=1
        )
        for q in range(p):
            g = g - dot(factor_ref[q, :, (p - q) * TILE:(p - q + 1) * TILE], above[q], (0, 0))
        above.append(dot(factor_ref[p, :, half:half + TILE], g, (1, 0)))
    above = jnp.concatenate(above, axis=0)
    update = dot(above, above, (0, 0))
    moved = rows_ref[...] - dot(first_ref[...], above, (1, 0))
    for t in range(panels):
        lanes = slice(t * TILE, (t + 1) * TILE)
        for p in range(panels):
            rows = slice(p * TILE, (p + 1) * TILE)
            if p <= t:
                work_ref[t, rows, :] = (
                    tile_of(gram_ref, rank, panels + p, panels + t, scale) - update[rows, lanes]
                )
            else:
                work_ref[t, rows, :] = jnp.zeros((TILE, TILE), jnp.float32)
        left_ref[t] = moved[:, lanes]
    out_ref[:, :half] = first_ref[...]

    def store(t, solved):
        lanes = slice(t * TILE, (t + 1) * TILE)
        out_ref[:, half + t * TILE:half + (t + 1) * TILE] = solved
        if rounded:
            round_ref[:, lanes] = solved.astype(jnp.bfloat16)

    factor_and_solve(work_ref, left_ref, panel_ref, spread_ref, store)


def orth_scratch(rows, half):
    return [
        pltpu.VMEM((half // TILE, half, TILE), jnp.float32),
        pltpu.VMEM((half // TILE, rows, TILE), jnp.float32),
        pltpu.VMEM((TILE, half + TILE), jnp.float32),
        pltpu.VMEM((2, SUB, SUB, TILE), jnp.float32),
    ]


def orth_left(matrix, gram, total_rows, rounded):
    rows, half = matrix.shape
    outs = [
        jax.ShapeDtypeStruct((rows, half), jnp.float32),
        jax.ShapeDtypeStruct((half // TILE, TILE, half + TILE), jnp.float32),
    ]
    if rounded:
        outs.insert(0, jax.ShapeDtypeStruct((rows, half), jnp.bfloat16))
    return pl.pallas_call(
        functools.partial(left_kernel, scale=1.0 / total_rows, rounded=rounded),
        out_shape=tuple(outs),
        scratch_shapes=orth_scratch(rows, half),
        compiler_params=pltpu.CompilerParams(vmem_limit_bytes=VMEM_BYTES),
        name="orth_left",
    )(gram, matrix)


def orth_right(matrix, gram, first, factor, total_rows, rounded):
    rows, half = matrix.shape
    outs = [jax.ShapeDtypeStruct((rows, 2 * half), jnp.float32)]
    if rounded:
        outs.insert(0, jax.ShapeDtypeStruct((rows, half), jnp.bfloat16))
    return pl.pallas_call(
        functools.partial(right_kernel, scale=1.0 / total_rows, rounded=rounded),
        out_shape=tuple(outs),
        scratch_shapes=orth_scratch(rows, half),
        compiler_params=pltpu.CompilerParams(vmem_limit_bytes=VMEM_BYTES),
        name="orth_right",
    )(gram, matrix, first, factor)


def along(axis, step):
    pairs = []
    for y in range(RING):
        for x in range(RING):
            for core in range(2):
                to = {
                    "y": ((y + step) % RING, x, core),
                    "x": (y, (x + step) % RING, core),
                    "core": (y, x, 1 - core),
                }[axis]
                pairs.append(((y * RING + x) * 2 + core, (to[0] * RING + to[1]) * 2 + to[2]))
    return pairs


def to_suf(value, step):
    return lax.ppermute(value, "suf", [(s, (s + step) % RING) for s in range(RING)])


def to_pre(value, axis, step=1):
    return lax.ppermute(value, "pre", along(axis, step))


def gather_suf(value):
    return jnp.concatenate([value] + [to_suf(value, -k) for k in range(1, RING)], axis=0)


def swap_chips(value):
    groups = [[chip * 2 + core for chip in range(RING * RING)] for core in range(2)]
    return lax.all_to_all(value, "pre", 0, 0, axis_index_groups=groups, tiled=True)


def tie(first, second):
    return lax.optimization_barrier((first, second))


def gather_chips(value):
    return swap_chips(jnp.broadcast_to(value[None], (RING * RING,) + value.shape))


def gather_cores(held, core):
    other = to_pre(held, "core")
    first = jnp.where(core == 0, held, other)
    second = jnp.where(core == 0, other, held)
    return jnp.stack([first, second], axis=1).reshape(-1, held.shape[-1])


def scatter_suf(chunks):
    moved = {k: to_suf(chunks[k], k) for k in (2, 1, 3)}
    return [chunks[0]] + [moved[k] for k in (1, 2, 3)]


def scatter_cores(partial_value, core):
    rows, columns = partial_value.shape
    chips = RING * RING
    held = partial_value.reshape(chips, 2, rows // (chips * 2), columns)
    mine = jnp.where(core == 0, held[:, 0], held[:, 1])
    theirs = jnp.where(core == 0, held[:, 1], held[:, 0])
    return mine + to_pre(theirs, "core")


def scatter_chips(held, axes, place):
    held = held.reshape((RING, RING) + held.shape[1:])
    if axes[0] == "x":
        held = jnp.swapaxes(held, 0, 1)
    for axis in axes:
        parts = []
        for k in range(RING):
            part = lax.dynamic_index_in_dim(held, (place[axis] + k) % RING, 0, keepdims=False)
            parts.append(part if k == 0 else to_pre(part, axis, k))
        held = sum(parts[1:], parts[0])
    return parts


def sum_all(gram, core):
    rows, lanes = gram.shape
    chips = RING * RING
    half = rows // 2
    low, high = gram[:half], gram[half:]
    mine = jnp.where(core == 0, low, high)
    mine = mine + to_pre(jnp.where(core == 0, high, low), "core")
    pieces = swap_chips(mine)
    piece = jnp.sum(pieces.reshape(chips, half // chips, lanes), axis=0)
    parts = [piece] + [to_suf(piece, k) for k in range(1, RING)]
    total = sum(parts[1:], parts[0])
    spread = jnp.broadcast_to(total[None], (chips,) + total.shape).reshape(half, lanes)
    mine = swap_chips(spread)
    other = to_pre(mine, "core")
    low = jnp.where(core == 0, mine, other)
    high = jnp.where(core == 0, other, mine)
    return jnp.concatenate([low, high], axis=0)


def local(values, block_rows, block_cols, block_count, test_matrix):
    pre, suf = lax.axis_index("pre"), lax.axis_index("suf")
    core = pre % 2
    place = {"y": pre // (2 * RING), "x": pre // 2 % RING}
    prefix_total = PB * BLK * lax.axis_size("pre")
    suffix_total = SB * BLK * lax.axis_size("suf")
    row_ids = ((block_rows[0] // RING - suf) % RING) * RING + block_rows[0] % RING
    dense = dense_blocks(values[0], row_ids, block_cols[0], block_count)
    prefix_share = PB * BLK // RING
    suffix_share = test_matrix.shape[0]

    def prefix_chunks(panel):
        chunks = [None] * RING
        for k in (2, 1, 3, 0):
            chunks[k] = jnp.dot(
                dense[k * prefix_share:(k + 1) * prefix_share], panel,
                preferred_element_type=jnp.float32,
            )
        return chunks

    def suffix_sums(panel):
        partial_value = lax.dot_general(
            dense, panel, (((0,), (0,)), ((), ())), preferred_element_type=jnp.float32
        )
        return scatter_cores(partial_value, core)

    held, dense = tie(gather_chips(test_matrix), dense)
    chunks = prefix_chunks(gather_cores(held, core))
    left, right, gram = sum_and_gram(scatter_suf(chunks), [], prefix_share)
    gram = sum_all(gram, core)

    rounded, first, factor = orth_left(left, gram, prefix_total, True)
    left = gather_suf(rounded)
    rounded, _ = orth_right(right, gram, first, factor, prefix_total, True)
    rounded, left = tie(rounded, left)
    right = gather_suf(rounded)
    left = suffix_sums(left)
    right, left = tie(right, left)
    left = scatter_chips(left, "yx", place)
    right = scatter_chips(suffix_sums(right), "xy", place)
    left, right, gram = sum_and_gram(left, right, suffix_share)
    gram = sum_all(gram, core)

    rounded, first, factor = orth_left(left, gram, suffix_total, True)
    left = gather_chips(rounded)
    rounded, suffix_basis = orth_right(right, gram, first, factor, suffix_total, True)
    rounded, left = tie(rounded, left)
    right = gather_chips(rounded)
    left = scatter_suf(prefix_chunks(gather_cores(left, core)))
    right, left[2] = tie(right, left[2])
    right = scatter_suf(prefix_chunks(gather_cores(right, core)))
    left, right, gram = sum_and_gram(left, right, prefix_share)
    gram = sum_all(gram, core)
    first, factor = orth_left(left, gram, prefix_total, False)
    (prefix_basis,) = orth_right(right, gram, first, factor, prefix_total, False)
    return (prefix_basis, suffix_basis)


def solution(mesh):
    in_specs = (
        P(("pre", "suf"), None, None, None),
        P(("pre", "suf"), None),
        P(("pre", "suf"), None),
        P(("pre", "suf")),
        P(("suf", "pre"), None),
    )
    out_specs = (P(("pre", "suf"), None), P(("suf", "pre"), None))
    return jax.shard_map(local, mesh=mesh, in_specs=in_specs, out_specs=out_specs, check_vma=False)
```

```python
import functools

import jax
import jax.numpy as jnp
from jax import lax
from jax.experimental import pallas as pl
from jax.experimental.pallas import tpu as pltpu
from jax.sharding import PartitionSpec as P

BLK = 128
PB = 16
SB = 16
TILE = 128
SUB = 8
STAGE = 8
RING = 4
VMEM_BYTES = 48 * 1024 * 1024

highest = lax.Precision.HIGHEST


def dense_kernel(count_ref, rows_ref, cols_ref, values_ref, out_ref, sem):
    out_ref[...] = jnp.zeros(out_ref.shape, out_ref.dtype)
    live = count_ref[0]

    def copy(k):
        row = pl.multiple_of(rows_ref[k] * BLK, BLK)
        col = pl.multiple_of(cols_ref[k] * BLK, BLK)
        return pltpu.make_async_copy(
            values_ref.at[k], out_ref.at[pl.ds(row, BLK), pl.ds(col, BLK)], sem
        )

    def start(k, carry):
        copy(k).start()
        return carry

    def wait(k, carry):
        copy(k).wait()
        return carry

    lax.fori_loop(0, live, start, 0)
    lax.fori_loop(0, live, wait, 0)


def dense_blocks(block_values, row_ids, col_ids, live_count):
    smem = pl.BlockSpec(memory_space=pltpu.SMEM)
    return pl.pallas_call(
        dense_kernel,
        out_shape=jax.ShapeDtypeStruct((PB * BLK, SB * BLK), jnp.bfloat16),
        in_specs=[smem, smem, smem, pl.BlockSpec(memory_space=pl.ANY)],
        out_specs=pl.BlockSpec(memory_space=pltpu.VMEM),
        scratch_shapes=[pltpu.SemaphoreType.DMA],
        compiler_params=pltpu.CompilerParams(vmem_limit_bytes=VMEM_BYTES),
        name="dense_blocks",
    )(live_count, row_ids, col_ids, block_values)


def tile_pairs(rank):
    panels = rank // TILE
    return [(p, t) for p in range(panels) for t in range(p, panels)]


def gram_kernel(*refs, count):
    parts, (left_ref, right_ref, gram_ref) = refs[:-3], refs[-3:]
    rows, half = left_ref.shape
    whole = len(parts) == count
    for total_ref, mine, lane in (
        (left_ref, parts[:count], 0), (right_ref, parts if whole else parts[count:], half if whole else 0)
    ):
        total = None
        for part in mine:
            for at in range(0, part.shape[0], rows):
                chunk = part[at:at + rows, lane:lane + half]
                total = chunk if total is None else total + chunk
        total_ref[...] = total
    total = jnp.concatenate([left_ref[...], right_ref[...]], axis=1)
    rank = 2 * half
    at = 0
    for p in range(rank // TILE):
        row = lax.dot_general(
            total[:, p * TILE:(p + 1) * TILE], total[:, p * TILE:], (((0,), (0,)), ((), ())),
            precision=highest, preferred_element_type=jnp.float32,
        )
        for t in range(rank // TILE - p):
            gram_ref[at:at + TILE, :] = row[:, t * TILE:(t + 1) * TILE]
            at += TILE


def sum_and_gram(left_parts, right_parts, rows):
    half = left_parts[0].shape[1] // (1 if right_parts else 2)
    packed = len(tile_pairs(2 * half)) * TILE
    share = jax.ShapeDtypeStruct((rows, half), jnp.float32)
    return pl.pallas_call(
        functools.partial(gram_kernel, count=len(left_parts)),
        out_shape=(share, share, jax.ShapeDtypeStruct((packed, TILE), jnp.float32)),
        compiler_params=pltpu.CompilerParams(vmem_limit_bytes=VMEM_BYTES),
        name="gram",
    )(*left_parts, *right_parts)


def eliminate(panel_ref, spread_ref):
    total = panel_ref.shape[1]
    tiles = total // TILE
    groups = TILE // SUB
    sub_ids = lax.broadcasted_iota(jnp.int32, (SUB, TILE), 0)
    for b in range(groups):
        base = b * SUB
        here = slice(base, base + SUB)
        square = panel_ref[here, here]
        slot = b % 2
        for j in range(SUB):
            spread_ref[slot, j] = jnp.broadcast_to(square[:, j:j + 1], (SUB, TILE))
        e = [
            [jnp.broadcast_to(spread_ref[slot, j, i:i + 1, :], (SUB, TILE)) for j in range(i + 1)]
            for i in range(SUB)
        ]
        if b + 1 < groups:
            below = panel_ref[base + SUB:base + 2 * SUB, here]
            raw = [jnp.broadcast_to(below[:, k:k + 1], (SUB, TILE)) for k in range(SUB)]
        inv = [None] * SUB
        for k in range(SUB):
            inv[k] = lax.rsqrt(e[k][k])
            for i in range(k + 1, SUB):
                e[i][k] = e[i][k] * inv[k]
            for i in range(k + 1, SUB):
                for j in range(k + 1, i + 1):
                    e[i][j] = e[i][j] - e[i][k] * e[j][k]
        r = []
        for k in range(SUB):
            row = []
            for t in range(tiles):
                v = jnp.broadcast_to(panel_ref[base + k:base + k + 1, t * TILE:(t + 1) * TILE], (SUB, TILE))
                for j in range(k):
                    v = v - e[k][j] * r[j][t]
                row.append(v * inv[k])
            r.append(row)
        for t in range(tiles):
            v = r[0][t]
            for k in range(1, SUB):
                v = jnp.where(sub_ids == k, r[k][t], v)
            panel_ref[here, t * TILE:(t + 1) * TILE] = v
            if t == 0:
                turned = v.T
        stage = (b // STAGE + 1) * STAGE
        for g in range(b + 1, stage):
            there = slice(g * SUB, (g + 1) * SUB)
            if g == b + 1:
                cols = []
                for k in range(SUB):
                    v = raw[k]
                    for j in range(k):
                        v = v - e[k][j] * cols[j]
                    cols.append(v * inv[k])
            else:
                cols = [jnp.broadcast_to(turned[there, k:k + 1], (SUB, TILE)) for k in range(SUB)]
            for t in range(tiles):
                v = panel_ref[there, t * TILE:(t + 1) * TILE]
                for k in range(SUB):
                    v = v - cols[k] * r[k][t]
                panel_ref[there, t * TILE:(t + 1) * TILE] = v
        if b + 1 == stage and stage < groups:
            done, low = slice((stage - STAGE) * SUB, stage * SUB), stage * SUB
            panel_ref[low:, :] = panel_ref[low:, :] - lax.dot_general(
                panel_ref[done, low:TILE], panel_ref[done, :], (((0,), (0,)), ((), ())),
                precision=highest, preferred_element_type=jnp.float32,
            )


def factor_and_solve(work_ref, left_ref, panel_ref, spread_ref, store):
    panels = work_ref.shape[0]
    rank = panels * TILE
    row_ids = lax.broadcasted_iota(jnp.int32, (TILE, TILE), 0)
    lane_ids = lax.broadcasted_iota(jnp.int32, (TILE, TILE), 1)
    unit = jnp.where(row_ids == lane_ids, 1.0, 0.0).astype(jnp.float32)

    def panel_step(p, carry):
        rows = pl.ds(pl.multiple_of(p * TILE, TILE), TILE)
        for t in range(panels):
            panel_ref[:, t * TILE:(t + 1) * TILE] = work_ref[(p + t) % panels, rows, :]
        panel_ref[:, rank:rank + TILE] = unit
        eliminate(panel_ref, spread_ref)
        solved = lax.dot_general(
            left_ref[p], panel_ref[:, rank:rank + TILE], (((1,), (1,)), ((), ())), precision=highest,
            preferred_element_type=jnp.float32,
        )
        for t in range(panels):
            @pl.when(p == t)
            def _():
                store(t, solved)

        @pl.when(p < panels - 1)
        def _():
            across = panel_ref[:, TILE:rank]
            moved = jnp.dot(solved, across, precision=highest, preferred_element_type=jnp.float32)
            update = lax.dot_general(
                across, across, (((0,), (0,)), ((), ())), precision=highest,
                preferred_element_type=jnp.float32,
            )
            for t in range(1, panels):
                tile = (p + t) % panels
                lanes = slice((t - 1) * TILE, t * TILE)
                left_ref[tile] = left_ref[tile] - moved[:, lanes]
                for u in range(1, panels):
                    under = pl.ds(pl.multiple_of((p + u) % panels * TILE, TILE), TILE)
                    work_ref[tile, under, :] = (
                        work_ref[tile, under, :] - update[(u - 1) * TILE:u * TILE, lanes]
                    )
        return carry

    lax.fori_loop(0, panels, panel_step, 0)


def tile_of(gram_ref, rank, p, t, scale):
    at = tile_pairs(rank).index((p, t)) * TILE
    return gram_ref[at:at + TILE, :] * scale


def left_kernel(gram_ref, rows_ref, *refs, scale, rounded):
    if rounded:
        round_ref, out_ref, factor_ref, work_ref, left_ref, panel_ref, spread_ref = refs
    else:
        out_ref, factor_ref, work_ref, left_ref, panel_ref, spread_ref = refs
    half = rows_ref.shape[1]
    panels = half // TILE
    for t in range(panels):
        lanes = slice(t * TILE, (t + 1) * TILE)
        for p in range(panels):
            rows = slice(p * TILE, (p + 1) * TILE)
            if p <= t:
                work_ref[t, rows, :] = tile_of(gram_ref, 2 * half, p, t, scale)
            else:
                work_ref[t, rows, :] = jnp.zeros((TILE, TILE), jnp.float32)
        left_ref[t] = rows_ref[:, lanes]

    def store(t, solved):
        lanes = slice(t * TILE, (t + 1) * TILE)
        out_ref[:, lanes] = solved
        if rounded:
            round_ref[:, lanes] = solved.astype(jnp.bfloat16)
        factor_ref[t] = panel_ref[...]

    factor_and_solve(work_ref, left_ref, panel_ref, spread_ref, store)


def right_kernel(gram_ref, rows_ref, first_ref, factor_ref, *refs, scale, rounded):
    if rounded:
        round_ref, out_ref, work_ref, left_ref, panel_ref, spread_ref = refs
    else:
        out_ref, work_ref, left_ref, panel_ref, spread_ref = refs
    half = rows_ref.shape[1]
    panels = half // TILE
    rank = 2 * half

    def dot(a, b, dims):
        return lax.dot_general(
            a, b, ((dims[:1], dims[1:]), ((), ())), precision=highest,
            preferred_element_type=jnp.float32,
        )

    above = []
    for p in range(panels):
        g = jnp.concatenate(
            [tile_of(gram_ref, rank, p, panels + t, scale) for t in range(panels)], axis=1
        )
        for q in range(p):
            g = g - dot(factor_ref[q, :, (p - q) * TILE:(p - q + 1) * TILE], above[q], (0, 0))
        above.append(dot(factor_ref[p, :, half:half + TILE], g, (1, 0)))
    above = jnp.concatenate(above, axis=0)
    update = dot(above, above, (0, 0))
    moved = rows_ref[...] - dot(first_ref[...], above, (1, 0))
    for t in range(panels):
        lanes = slice(t * TILE, (t + 1) * TILE)
        for p in range(panels):
            rows = slice(p * TILE, (p + 1) * TILE)
            if p <= t:
                work_ref[t, rows, :] = (
                    tile_of(gram_ref, rank, panels + p, panels + t, scale) - update[rows, lanes]
                )
            else:
                work_ref[t, rows, :] = jnp.zeros((TILE, TILE), jnp.float32)
        left_ref[t] = moved[:, lanes]
    out_ref[:, :half] = first_ref[...]

    def store(t, solved):
        lanes = slice(t * TILE, (t + 1) * TILE)
        out_ref[:, half + t * TILE:half + (t + 1) * TILE] = solved
        if rounded:
            round_ref[:, lanes] = solved.astype(jnp.bfloat16)

    factor_and_solve(work_ref, left_ref, panel_ref, spread_ref, store)


def orth_scratch(rows, half):
    return [
        pltpu.VMEM((half // TILE, half, TILE), jnp.float32),
        pltpu.VMEM((half // TILE, rows, TILE), jnp.float32),
        pltpu.VMEM((TILE, half + TILE), jnp.float32),
        pltpu.VMEM((2, SUB, SUB, TILE), jnp.float32),
    ]


def orth_left(matrix, gram, total_rows, rounded):
    rows, half = matrix.shape
    outs = [
        jax.ShapeDtypeStruct((rows, half), jnp.float32),
        jax.ShapeDtypeStruct((half // TILE, TILE, half + TILE), jnp.float32),
    ]
    if rounded:
        outs.insert(0, jax.ShapeDtypeStruct((rows, half), jnp.bfloat16))
    return pl.pallas_call(
        functools.partial(left_kernel, scale=1.0 / total_rows, rounded=rounded),
        out_shape=tuple(outs),
        scratch_shapes=orth_scratch(rows, half),
        compiler_params=pltpu.CompilerParams(vmem_limit_bytes=VMEM_BYTES),
        name="orth_left",
    )(gram, matrix)


def orth_right(matrix, gram, first, factor, total_rows, rounded):
    rows, half = matrix.shape
    outs = [jax.ShapeDtypeStruct((rows, 2 * half), jnp.float32)]
    if rounded:
        outs.insert(0, jax.ShapeDtypeStruct((rows, half), jnp.bfloat16))
    return pl.pallas_call(
        functools.partial(right_kernel, scale=1.0 / total_rows, rounded=rounded),
        out_shape=tuple(outs),
        scratch_shapes=orth_scratch(rows, half),
        compiler_params=pltpu.CompilerParams(vmem_limit_bytes=VMEM_BYTES),
        name="orth_right",
    )(gram, matrix, first, factor)


def along(axis, step):
    pairs = []
    for y in range(RING):
        for x in range(RING):
            for core in range(2):
                to = {
                    "y": ((y + step) % RING, x, core),
                    "x": (y, (x + step) % RING, core),
                    "core": (y, x, 1 - core),
                }[axis]
                pairs.append(((y * RING + x) * 2 + core, (to[0] * RING + to[1]) * 2 + to[2]))
    return pairs


def to_suf(value, step):
    return lax.ppermute(value, "suf", [(s, (s + step) % RING) for s in range(RING)])


def to_pre(value, axis, step=1):
    return lax.ppermute(value, "pre", along(axis, step))


def gather_suf(value):
    return jnp.concatenate([value] + [to_suf(value, -k) for k in range(1, RING)], axis=0)


def swap_chips(value):
    groups = [[chip * 2 + core for chip in range(RING * RING)] for core in range(2)]
    return lax.all_to_all(value, "pre", 0, 0, axis_index_groups=groups, tiled=True)


def tie(first, second):
    return lax.optimization_barrier((first, second))


def gather_chips(value):
    return swap_chips(jnp.broadcast_to(value[None], (RING * RING,) + value.shape))


def gather_cores(held, core):
    other = to_pre(held, "core")
    first = jnp.where(core == 0, held, other)
    second = jnp.where(core == 0, other, held)
    return jnp.stack([first, second], axis=1).reshape(-1, held.shape[-1])


def scatter_suf(chunks):
    moved = {k: to_suf(chunks[k], k) for k in (2, 1, 3)}
    return [chunks[0]] + [moved[k] for k in (1, 2, 3)]


def scatter_cores(partial_value, core):
    rows, columns = partial_value.shape
    chips = RING * RING
    held = partial_value.reshape(chips, 2, rows // (chips * 2), columns)
    mine = jnp.where(core == 0, held[:, 0], held[:, 1])
    theirs = jnp.where(core == 0, held[:, 1], held[:, 0])
    return mine + to_pre(theirs, "core")


def scatter_chips(held, axes, place):
    held = held.reshape((RING, RING) + held.shape[1:])
    if axes[0] == "x":
        held = jnp.swapaxes(held, 0, 1)
    for axis in axes:
        parts = []
        for k in range(RING):
            part = lax.dynamic_index_in_dim(held, (place[axis] + k) % RING, 0, keepdims=False)
            parts.append(part if k == 0 else to_pre(part, axis, k))
        held = sum(parts[1:], parts[0])
    return parts


def sum_all(gram, core):
    rows, lanes = gram.shape
    chips = RING * RING
    half = rows // 2
    low, high = gram[:half], gram[half:]
    mine = jnp.where(core == 0, low, high)
    mine = mine + to_pre(jnp.where(core == 0, high, low), "core")
    pieces = swap_chips(mine)
    piece = jnp.sum(pieces.reshape(chips, half // chips, lanes), axis=0)
    parts = [piece] + [to_suf(piece, k) for k in range(1, RING)]
    total = sum(parts[1:], parts[0])
    spread = jnp.broadcast_to(total[None], (chips,) + total.shape).reshape(half, lanes)
    mine = swap_chips(spread)
    other = to_pre(mine, "core")
    low = jnp.where(core == 0, mine, other)
    high = jnp.where(core == 0, other, mine)
    return jnp.concatenate([low, high], axis=0)


def local(values, block_rows, block_cols, block_count, test_matrix):
    pre, suf = lax.axis_index("pre"), lax.axis_index("suf")
    core = pre % 2
    place = {"y": pre // (2 * RING), "x": pre // 2 % RING}
    prefix_total = PB * BLK * lax.axis_size("pre")
    suffix_total = SB * BLK * lax.axis_size("suf")
    row_ids = ((block_rows[0] // RING - suf) % RING) * RING + block_rows[0] % RING
    dense = dense_blocks(values[0], row_ids, block_cols[0], block_count)
    prefix_share = PB * BLK // RING
    suffix_share = test_matrix.shape[0]

    def prefix_chunks(panel):
        chunks = [None] * RING
        for k in (2, 1, 3, 0):
            chunks[k] = jnp.dot(
                dense[k * prefix_share:(k + 1) * prefix_share], panel,
                preferred_element_type=jnp.float32,
            )
        return chunks

    def suffix_sums(panel):
        partial_value = lax.dot_general(
            dense, panel, (((0,), (0,)), ((), ())), preferred_element_type=jnp.float32
        )
        return scatter_cores(partial_value, core)

    held, dense = tie(gather_chips(test_matrix), dense)
    chunks = prefix_chunks(gather_cores(held, core))
    left, right, gram = sum_and_gram(scatter_suf(chunks), [], prefix_share)
    gram = sum_all(gram, core)

    rounded, first, factor = orth_left(left, gram, prefix_total, True)
    left = gather_suf(rounded)
    rounded, _ = orth_right(right, gram, first, factor, prefix_total, True)
    rounded, left = tie(rounded, left)
    right = gather_suf(rounded)
    left = suffix_sums(left)
    right, left = tie(right, left)
    left = scatter_chips(left, "yx", place)
    right = scatter_chips(suffix_sums(right), "xy", place)
    left, right, gram = sum_and_gram(left, right, suffix_share)
    gram = sum_all(gram, core)

    rounded, first, factor = orth_left(left, gram, suffix_total, True)
    left = gather_chips(rounded)
    rounded, suffix_basis = orth_right(right, gram, first, factor, suffix_total, True)
    rounded, left = tie(rounded, left)
    right = gather_chips(rounded)
    left = scatter_suf(prefix_chunks(gather_cores(left, core)))
    right, left[2] = tie(right, left[2])
    right = scatter_suf(prefix_chunks(gather_cores(right, core)))
    left, right, gram = sum_and_gram(left, right, prefix_share)
    gram = sum_all(gram, core)
    first, factor = orth_left(left, gram, prefix_total, False)
    (prefix_basis,) = orth_right(right, gram, first, factor, prefix_total, False)
    return (prefix_basis, suffix_basis)


def solution(mesh):
    in_specs = (
        P(("pre", "suf"), None, None, None),
        P(("pre", "suf"), None),
        P(("pre", "suf"), None),
        P(("pre", "suf")),
        P(("suf", "pre"), None),
    )
    out_specs = (P(("pre", "suf"), None), P(("suf", "pre"), None))
    return jax.shard_map(local, mesh=mesh, in_specs=in_specs, out_specs=out_specs, check_vma=False)
```

```python
import functools

import jax
import jax.numpy as jnp
from jax import lax
from jax.experimental import pallas as pl
from jax.experimental.pallas import tpu as pltpu
from jax.sharding import PartitionSpec as P

BLK = 128
PB = 16
SB = 16
TILE = 128
SUB = 8
STAGE = 8
RING = 4
VMEM_BYTES = 20 * 1024 * 1024

highest = lax.Precision.HIGHEST


def dense_kernel(count_ref, rows_ref, cols_ref, values_ref, out_ref, sem):
    out_ref[...] = jnp.zeros(out_ref.shape, out_ref.dtype)
    live = count_ref[0]

    def copy(k):
        row = pl.multiple_of(rows_ref[k] * BLK, BLK)
        col = pl.multiple_of(cols_ref[k] * BLK, BLK)
        return pltpu.make_async_copy(
            values_ref.at[k], out_ref.at[pl.ds(row, BLK), pl.ds(col, BLK)], sem
        )

    def start(k, carry):
        copy(k).start()
        return carry

    def wait(k, carry):
        copy(k).wait()
        return carry

    lax.fori_loop(0, live, start, 0)
    lax.fori_loop(0, live, wait, 0)


def dense_blocks(block_values, row_ids, col_ids, live_count):
    smem = pl.BlockSpec(memory_space=pltpu.SMEM)
    return pl.pallas_call(
        dense_kernel,
        out_shape=jax.ShapeDtypeStruct((PB * BLK, SB * BLK), jnp.bfloat16),
        in_specs=[smem, smem, smem, pl.BlockSpec(memory_space=pl.ANY)],
        out_specs=pl.BlockSpec(memory_space=pltpu.VMEM),
        scratch_shapes=[pltpu.SemaphoreType.DMA],
        compiler_params=pltpu.CompilerParams(vmem_limit_bytes=VMEM_BYTES),
        name="dense_blocks",
    )(live_count, row_ids, col_ids, block_values)


def tile_pairs(rank):
    panels = rank // TILE
    return [(p, t) for p in range(panels) for t in range(p, panels)]


def gram_kernel(*refs, count):
    parts, (left_ref, right_ref, gram_ref) = refs[:-3], refs[-3:]
    rows, half = left_ref.shape
    whole = len(parts) == count
    for total_ref, mine, lane in (
        (left_ref, parts[:count], 0), (right_ref, parts if whole else parts[count:], half if whole else 0)
    ):
        total = None
        for part in mine:
            for at in range(0, part.shape[0], rows):
                chunk = part[at:at + rows, lane:lane + half]
                total = chunk if total is None else total + chunk
        total_ref[...] = total
    total = jnp.concatenate([left_ref[...], right_ref[...]], axis=1)
    rank = 2 * half
    at = 0
    for p in range(rank // TILE):
        row = lax.dot_general(
            total[:, p * TILE:(p + 1) * TILE], total[:, p * TILE:], (((0,), (0,)), ((), ())),
            precision=highest, preferred_element_type=jnp.float32,
        )
        for t in range(rank // TILE - p):
            gram_ref[at:at + TILE, :] = row[:, t * TILE:(t + 1) * TILE]
            at += TILE


def sum_and_gram(left_parts, right_parts, rows):
    half = left_parts[0].shape[1] // (1 if right_parts else 2)
    packed = len(tile_pairs(2 * half)) * TILE
    share = jax.ShapeDtypeStruct((rows, half), jnp.float32)
    return pl.pallas_call(
        functools.partial(gram_kernel, count=len(left_parts)),
        out_shape=(share, share, jax.ShapeDtypeStruct((packed, TILE), jnp.float32)),
        compiler_params=pltpu.CompilerParams(vmem_limit_bytes=VMEM_BYTES),
        name="gram",
    )(*left_parts, *right_parts)


def eliminate(panel_ref, spread_ref):
    total = panel_ref.shape[1]
    tiles = total // TILE
    groups = TILE // SUB
    sub_ids = lax.broadcasted_iota(jnp.int32, (SUB, TILE), 0)
    for b in range(groups):
        base = b * SUB
        here = slice(base, base + SUB)
        square = panel_ref[here, here]
        slot = b % 2
        for j in range(SUB):
            spread_ref[slot, j] = jnp.broadcast_to(square[:, j:j + 1], (SUB, TILE))
        e = [
            [jnp.broadcast_to(spread_ref[slot, j, i:i + 1, :], (SUB, TILE)) for j in range(i + 1)]
            for i in range(SUB)
        ]
        if b + 1 < groups:
            below = panel_ref[base + SUB:base + 2 * SUB, here]
            raw = [jnp.broadcast_to(below[:, k:k + 1], (SUB, TILE)) for k in range(SUB)]
        inv = [None] * SUB
        for k in range(SUB):
            inv[k] = lax.rsqrt(e[k][k])
            for i in range(k + 1, SUB):
                e[i][k] = e[i][k] * inv[k]
            for i in range(k + 1, SUB):
                for j in range(k + 1, i + 1):
                    e[i][j] = e[i][j] - e[i][k] * e[j][k]
        r = []
        for k in range(SUB):
            row = []
            for t in range(tiles):
                v = jnp.broadcast_to(panel_ref[base + k:base + k + 1, t * TILE:(t + 1) * TILE], (SUB, TILE))
                for j in range(k):
                    v = v - e[k][j] * r[j][t]
                row.append(v * inv[k])
            r.append(row)
        for t in range(tiles):
            v = r[0][t]
            for k in range(1, SUB):
                v = jnp.where(sub_ids == k, r[k][t], v)
            panel_ref[here, t * TILE:(t + 1) * TILE] = v
            if t == 0:
                turned = v.T
        stage = (b // STAGE + 1) * STAGE
        for g in range(b + 1, stage):
            there = slice(g * SUB, (g + 1) * SUB)
            if g == b + 1:
                cols = []
                for k in range(SUB):
                    v = raw[k]
                    for j in range(k):
                        v = v - e[k][j] * cols[j]
                    cols.append(v * inv[k])
            else:
                cols = [jnp.broadcast_to(turned[there, k:k + 1], (SUB, TILE)) for k in range(SUB)]
            for t in range(tiles):
                v = panel_ref[there, t * TILE:(t + 1) * TILE]
                for k in range(SUB):
                    v = v - cols[k] * r[k][t]
                panel_ref[there, t * TILE:(t + 1) * TILE] = v
        if b + 1 == stage and stage < groups:
            done, low = slice((stage - STAGE) * SUB, stage * SUB), stage * SUB
            panel_ref[low:, :] = panel_ref[low:, :] - lax.dot_general(
                panel_ref[done, low:TILE], panel_ref[done, :], (((0,), (0,)), ((), ())),
                precision=highest, preferred_element_type=jnp.float32,
            )


def factor_and_solve(work_ref, left_ref, panel_ref, spread_ref, store):
    panels = work_ref.shape[0]
    rank = panels * TILE
    row_ids = lax.broadcasted_iota(jnp.int32, (TILE, TILE), 0)
    lane_ids = lax.broadcasted_iota(jnp.int32, (TILE, TILE), 1)
    unit = jnp.where(row_ids == lane_ids, 1.0, 0.0).astype(jnp.float32)

    def panel_step(p, carry):
        rows = pl.ds(pl.multiple_of(p * TILE, TILE), TILE)
        for t in range(panels):
            panel_ref[:, t * TILE:(t + 1) * TILE] = work_ref[(p + t) % panels, rows, :]
        panel_ref[:, rank:rank + TILE] = unit
        eliminate(panel_ref, spread_ref)
        solved = lax.dot_general(
            left_ref[p], panel_ref[:, rank:rank + TILE], (((1,), (1,)), ((), ())), precision=highest,
            preferred_element_type=jnp.float32,
        )
        for t in range(panels):
            @pl.when(p == t)
            def _():
                store(t, solved)

        @pl.when(p < panels - 1)
        def _():
            across = panel_ref[:, TILE:rank]
            moved = jnp.dot(solved, across, precision=highest, preferred_element_type=jnp.float32)
            update = lax.dot_general(
                across, across, (((0,), (0,)), ((), ())), precision=highest,
                preferred_element_type=jnp.float32,
            )
            for t in range(1, panels):
                tile = (p + t) % panels
                lanes = slice((t - 1) * TILE, t * TILE)
                left_ref[tile] = left_ref[tile] - moved[:, lanes]
                for u in range(1, panels):
                    under = pl.ds(pl.multiple_of((p + u) % panels * TILE, TILE), TILE)
                    work_ref[tile, under, :] = (
                        work_ref[tile, under, :] - update[(u - 1) * TILE:u * TILE, lanes]
                    )
        return carry

    lax.fori_loop(0, panels, panel_step, 0)


def tile_of(gram_ref, rank, p, t, scale):
    at = tile_pairs(rank).index((p, t)) * TILE
    return gram_ref[at:at + TILE, :] * scale


def left_kernel(gram_ref, rows_ref, *refs, scale, rounded):
    if rounded:
        round_ref, out_ref, factor_ref, work_ref, left_ref, panel_ref, spread_ref = refs
    else:
        out_ref, factor_ref, work_ref, left_ref, panel_ref, spread_ref = refs
    half = rows_ref.shape[1]
    panels = half // TILE
    for t in range(panels):
        lanes = slice(t * TILE, (t + 1) * TILE)
        for p in range(panels):
            rows = slice(p * TILE, (p + 1) * TILE)
            if p <= t:
                work_ref[t, rows, :] = tile_of(gram_ref, 2 * half, p, t, scale)
            else:
                work_ref[t, rows, :] = jnp.zeros((TILE, TILE), jnp.float32)
        left_ref[t] = rows_ref[:, lanes]

    def store(t, solved):
        lanes = slice(t * TILE, (t + 1) * TILE)
        out_ref[:, lanes] = solved
        if rounded:
            round_ref[:, lanes] = solved.astype(jnp.bfloat16)
        factor_ref[t] = panel_ref[...]

    factor_and_solve(work_ref, left_ref, panel_ref, spread_ref, store)


def right_kernel(gram_ref, rows_ref, first_ref, factor_ref, *refs, scale, rounded):
    if rounded:
        round_ref, out_ref, work_ref, left_ref, panel_ref, spread_ref = refs
    else:
        out_ref, work_ref, left_ref, panel_ref, spread_ref = refs
    half = rows_ref.shape[1]
    panels = half // TILE
    rank = 2 * half

    def dot(a, b, dims):
        return lax.dot_general(
            a, b, ((dims[:1], dims[1:]), ((), ())), precision=highest,
            preferred_element_type=jnp.float32,
        )

    above = []
    for p in range(panels):
        g = jnp.concatenate(
            [tile_of(gram_ref, rank, p, panels + t, scale) for t in range(panels)], axis=1
        )
        for q in range(p):
            g = g - dot(factor_ref[q, :, (p - q) * TILE:(p - q + 1) * TILE], above[q], (0, 0))
        above.append(dot(factor_ref[p, :, half:half + TILE], g, (1, 0)))
    above = jnp.concatenate(above, axis=0)
    update = dot(above, above, (0, 0))
    moved = rows_ref[...] - dot(first_ref[...], above, (1, 0))
    for t in range(panels):
        lanes = slice(t * TILE, (t + 1) * TILE)
        for p in range(panels):
            rows = slice(p * TILE, (p + 1) * TILE)
            if p <= t:
                work_ref[t, rows, :] = (
                    tile_of(gram_ref, rank, panels + p, panels + t, scale) - update[rows, lanes]
                )
            else:
                work_ref[t, rows, :] = jnp.zeros((TILE, TILE), jnp.float32)
        left_ref[t] = moved[:, lanes]
    out_ref[:, :half] = first_ref[...]

    def store(t, solved):
        lanes = slice(t * TILE, (t + 1) * TILE)
        out_ref[:, half + t * TILE:half + (t + 1) * TILE] = solved
        if rounded:
            round_ref[:, lanes] = solved.astype(jnp.bfloat16)

    factor_and_solve(work_ref, left_ref, panel_ref, spread_ref, store)


def orth_scratch(rows, half):
    return [
        pltpu.VMEM((half // TILE, half, TILE), jnp.float32),
        pltpu.VMEM((half // TILE, rows, TILE), jnp.float32),
        pltpu.VMEM((TILE, half + TILE), jnp.float32),
        pltpu.VMEM((2, SUB, SUB, TILE), jnp.float32),
    ]


def orth_left(matrix, gram, total_rows, rounded):
    rows, half = matrix.shape
    outs = [
        jax.ShapeDtypeStruct((rows, half), jnp.float32),
        jax.ShapeDtypeStruct((half // TILE, TILE, half + TILE), jnp.float32),
    ]
    if rounded:
        outs.insert(0, jax.ShapeDtypeStruct((rows, half), jnp.bfloat16))
    return pl.pallas_call(
        functools.partial(left_kernel, scale=1.0 / total_rows, rounded=rounded),
        out_shape=tuple(outs),
        scratch_shapes=orth_scratch(rows, half),
        compiler_params=pltpu.CompilerParams(vmem_limit_bytes=VMEM_BYTES),
        name="orth_left",
    )(gram, matrix)


def orth_right(matrix, gram, first, factor, total_rows, rounded):
    rows, half = matrix.shape
    outs = [jax.ShapeDtypeStruct((rows, 2 * half), jnp.float32)]
    if rounded:
        outs.insert(0, jax.ShapeDtypeStruct((rows, half), jnp.bfloat16))
    return pl.pallas_call(
        functools.partial(right_kernel, scale=1.0 / total_rows, rounded=rounded),
        out_shape=tuple(outs),
        scratch_shapes=orth_scratch(rows, half),
        compiler_params=pltpu.CompilerParams(vmem_limit_bytes=VMEM_BYTES),
        name="orth_right",
    )(gram, matrix, first, factor)


def along(axis, step):
    pairs = []
    for y in range(RING):
        for x in range(RING):
            for core in range(2):
                to = {
                    "y": ((y + step) % RING, x, core),
                    "x": (y, (x + step) % RING, core),
                    "core": (y, x, 1 - core),
                }[axis]
                pairs.append(((y * RING + x) * 2 + core, (to[0] * RING + to[1]) * 2 + to[2]))
    return pairs


def to_suf(value, step):
    return lax.ppermute(value, "suf", [(s, (s + step) % RING) for s in range(RING)])


def to_pre(value, axis, step=1):
    return lax.ppermute(value, "pre", along(axis, step))


def gather_suf(value):
    return jnp.concatenate([value] + [to_suf(value, -k) for k in range(1, RING)], axis=0)


def swap_chips(value):
    groups = [[chip * 2 + core for chip in range(RING * RING)] for core in range(2)]
    return lax.all_to_all(value, "pre", 0, 0, axis_index_groups=groups, tiled=True)


def tie(first, second):
    return lax.optimization_barrier((first, second))


def gather_chips(value):
    return swap_chips(jnp.broadcast_to(value[None], (RING * RING,) + value.shape))


def gather_cores(held, core):
    other = to_pre(held, "core")
    first = jnp.where(core == 0, held, other)
    second = jnp.where(core == 0, other, held)
    return jnp.stack([first, second], axis=1).reshape(-1, held.shape[-1])


def scatter_suf(chunks):
    moved = {k: to_suf(chunks[k], k) for k in (2, 1, 3)}
    return [chunks[0]] + [moved[k] for k in (1, 2, 3)]


def scatter_cores(partial_value, core):
    rows, columns = partial_value.shape
    chips = RING * RING
    held = partial_value.reshape(chips, 2, rows // (chips * 2), columns)
    mine = jnp.where(core == 0, held[:, 0], held[:, 1])
    theirs = jnp.where(core == 0, held[:, 1], held[:, 0])
    return mine + to_pre(theirs, "core")


def scatter_chips(held, axes, place):
    held = held.reshape((RING, RING) + held.shape[1:])
    if axes[0] == "x":
        held = jnp.swapaxes(held, 0, 1)
    for axis in axes:
        parts = []
        for k in range(RING):
            part = lax.dynamic_index_in_dim(held, (place[axis] + k) % RING, 0, keepdims=False)
            parts.append(part if k == 0 else to_pre(part, axis, k))
        held = sum(parts[1:], parts[0])
    return parts


def sum_all(gram, core):
    rows, lanes = gram.shape
    chips = RING * RING
    half = rows // 2
    low, high = gram[:half], gram[half:]
    mine = jnp.where(core == 0, low, high)
    mine = mine + to_pre(jnp.where(core == 0, high, low), "core")
    pieces = swap_chips(mine)
    piece = jnp.sum(pieces.reshape(chips, half // chips, lanes), axis=0)
    parts = [piece] + [to_suf(piece, k) for k in range(1, RING)]
    total = sum(parts[1:], parts[0])
    spread = jnp.broadcast_to(total[None], (chips,) + total.shape).reshape(half, lanes)
    mine = swap_chips(spread)
    other = to_pre(mine, "core")
    low = jnp.where(core == 0, mine, other)
    high = jnp.where(core == 0, other, mine)
    return jnp.concatenate([low, high], axis=0)


def local(values, block_rows, block_cols, block_count, test_matrix):
    pre, suf = lax.axis_index("pre"), lax.axis_index("suf")
    core = pre % 2
    place = {"y": pre // (2 * RING), "x": pre // 2 % RING}
    prefix_total = PB * BLK * lax.axis_size("pre")
    suffix_total = SB * BLK * lax.axis_size("suf")
    row_ids = ((block_rows[0] // RING - suf) % RING) * RING + block_rows[0] % RING
    dense = dense_blocks(values[0], row_ids, block_cols[0], block_count)
    prefix_share = PB * BLK // RING
    suffix_share = test_matrix.shape[0]

    def prefix_chunks(panel):
        chunks = [None] * RING
        for k in (2, 1, 3, 0):
            chunks[k] = jnp.dot(
                dense[k * prefix_share:(k + 1) * prefix_share], panel,
                preferred_element_type=jnp.float32,
            )
        return chunks

    def suffix_sums(panel):
        partial_value = lax.dot_general(
            dense, panel, (((0,), (0,)), ((), ())), preferred_element_type=jnp.float32
        )
        return scatter_cores(partial_value, core)

    chunks = prefix_chunks(gather_cores(gather_chips(test_matrix), core))
    left, right, gram = sum_and_gram(scatter_suf(chunks), [], prefix_share)
    gram = sum_all(gram, core)

    rounded, first, factor = orth_left(left, gram, prefix_total, True)
    left = gather_suf(rounded)
    rounded, _ = orth_right(right, gram, first, factor, prefix_total, True)
    rounded, left = tie(rounded, left)
    right = gather_suf(rounded)
    left = suffix_sums(left)
    right, left = tie(right, left)
    left = scatter_chips(left, "yx", place)
    right = scatter_chips(suffix_sums(right), "xy", place)
    left, right, gram = sum_and_gram(left, right, suffix_share)
    gram = sum_all(gram, core)

    rounded, first, factor = orth_left(left, gram, suffix_total, True)
    left = gather_chips(rounded)
    rounded, suffix_basis = orth_right(right, gram, first, factor, suffix_total, True)
    rounded, left = tie(rounded, left)
    right = gather_chips(rounded)
    left = scatter_suf(prefix_chunks(gather_cores(left, core)))
    right, left[2] = tie(right, left[2])
    right = scatter_suf(prefix_chunks(gather_cores(right, core)))
    left, right, gram = sum_and_gram(left, right, prefix_share)
    gram = sum_all(gram, core)
    first, factor = orth_left(left, gram, prefix_total, False)
    (prefix_basis,) = orth_right(right, gram, first, factor, prefix_total, False)
    return (prefix_basis, suffix_basis)


def solution(mesh):
    in_specs = (
        P(("pre", "suf"), None, None, None),
        P(("pre", "suf"), None),
        P(("pre", "suf"), None),
        P(("pre", "suf")),
        P(("suf", "pre"), None),
    )
    out_specs = (P(("pre", "suf"), None), P(("suf", "pre"), None))
    return jax.shard_map(local, mesh=mesh, in_specs=in_specs, out_specs=out_specs, check_vma=False)
```
